256 devices in a mesh: depth: 4 (over y_hi, core), row: 8 (over z), col: 8 (over y_lo, x).
Axes of the slice: x: 4, y: 4 (y_hi: 2, y_lo: 2; y = y_hi * 2 + y_lo), z: 8, core: 2. Of those that a mesh axis runs over, the one named last changes fastest.
Arguments:
- activations: bfloat16 [20480, 2048], P(('depth', 'row'), 'col'), may hold values from -6 to 6
- weight_in: bfloat16 [2048, 8192], P('row', 'col'), may hold values from -0.125 to 0.125
- weight_out: bfloat16 [8192, 2048], P('col', 'row'), may hold values from -0.0625 to 0.0625
- upstream: bfloat16 [20480, 2048], P(('depth', 'row'), 'col'), may hold values from -0.59765625 to 0.59765625
Outputs:
- grad_input: bfloat16 [20480, 2048], P(('depth', 'row'), 'col')
- grad_weight_in: float32 [2048, 8192], P('row', 'col')
- grad_weight_out: float32 [8192, 2048], P('col', 'row')
The draws below stay inside these ranges and needn't reach their ends.
All inputs are finite; a program needn't handle non-finite values.
Results may differ from the reference program's by a relative error of at most 0.022.
Values may be sent and summed in bfloat16 or wider, within the bound.
No kernel may reach another device: no remote copies, remote signals or barrier semaphores. Data moves between devices by JAX's collectives and lax.ppermute only.
A program may use at most 128 MiB of HBM per device.

```python
import jax
import jax.numpy as jnp
from jax import lax

D = 2048
FF = 8192
TOK_DEV = 640
TOKENS = 20480


def shard_levels(stream_key, dims, shards, least, high):
    def one(position, parts):
        heights = jax.random.uniform(jax.random.fold_in(jax.random.fold_in(stream_key, 6), position), (parts,), jnp.float32, least / len(shards), high / len(shards))
        return jnp.repeat(jnp.exp(heights), dims[position] // parts).reshape((-1,) + (1,) * (len(dims) - position - 1))

    level = one(*shards[0])
    for cut in shards[1:]:
        level = level * one(*cut)
    return level


def gaussian(key, dims, width, limit, shards=(), held_as=jnp.bfloat16):
    level = shard_levels(key, dims, shards, -0.22, 0.18) if shards else 1.0
    entries = jax.random.normal(key, dims, jnp.float32) * width * level
    return jnp.minimum(jnp.maximum(entries, -limit), limit).astype(held_as)


def setup_inputs(seed: int = 0) -> dict:
    key_of = jax.random.split(jax.random.key(seed), 5)
    activations = gaussian(key_of[0], (TOKENS, D), 1.0, 6.0, ((0, 32), (1, 8)))
    weight_in = gaussian(key_of[1], (D, FF), D ** -0.5, 0.125, ((0, 8), (1, 8)))
    weight_out = gaussian(key_of[2], (FF, D), FF ** -0.5, 0.0625, ((0, 8), (1, 8)))
    upstream = gaussian(key_of[3], (TOKENS, D), 0.1, 0.59765625, ((0, 32), (1, 8)))
    return {"activations": activations, "weight_in": weight_in, "weight_out": weight_out, "upstream": upstream}


def gelu_tanh(values):
    return jax.nn.gelu(values, approximate=True)

def reference(activations, weight_in, weight_out, upstream):
    pre = jnp.dot(activations, weight_in, preferred_element_type=jnp.float32)
    back = lax.dot_general(upstream, weight_out, (((1,), (1,)), ((), ())), preferred_element_type=jnp.float32)
    act_full, pull = jax.vjp(gelu_tanh, pre)
    dpre = pull(back)[0].astype(jnp.bfloat16)
    act = act_full.astype(jnp.bfloat16)
    grad_input = lax.dot_general(dpre, weight_in, (((1,), (1,)), ((), ())), preferred_element_type=jnp.float32).astype(jnp.bfloat16)
    blocks = TOKENS // TOK_DEV
    items = (activations.reshape(blocks, TOK_DEV, D), upstream.reshape(blocks, TOK_DEV, D), dpre.reshape(blocks, TOK_DEV, FF), act.reshape(blocks, TOK_DEV, FF))

    def accumulate(carry, item):
        inputs, grads, dpre_block, act_block = item
        first = lax.dot_general(inputs, dpre_block, (((0,), (0,)), ((), ())), preferred_element_type=jnp.float32)
        second = lax.dot_general(act_block, grads, (((0,), (0,)), ((), ())), preferred_element_type=jnp.float32)
        first = lax.optimization_barrier(first.astype(jnp.bfloat16)).astype(jnp.float32)
        second = lax.optimization_barrier(second.astype(jnp.bfloat16)).astype(jnp.float32)
        return ((carry[0] + first, carry[1] + second), None)
    start = (jnp.zeros((D, FF), jnp.float32), jnp.zeros((FF, D), jnp.float32))
    sums, unused = lax.scan(accumulate, start, items)
    return (grad_input, sums[0], sums[1])
```

```python
import functools

import jax
import jax.numpy as jnp
from jax import lax
from jax.experimental import pallas as pl
from jax.experimental.pallas import tpu as pltpu
from jax.sharding import PartitionSpec as P

VMEM_LIMIT = 56 * 1024 * 1024
ROOT_2_PI = 0.7978845608028654
CUBIC = 0.044715

CORE = [(d, d ^ 1) for d in range(4)]
Y_HI = [(d, d ^ 2) for d in range(4)]
Y_LO = [(c, c ^ 4) for c in range(8)]


def along_x(step):
    return [(c, (c & 4) | ((c + step) & 3)) for c in range(8)]


def forward_kernel(col_ref, *refs, chunks, tokens, part, half):
    own, sib = refs[:chunks], refs[chunks : 2 * chunks]
    weights, dpre_ref, grads_ref = refs[2 * chunks : 2 * chunks + 3]
    x_all, g_all, w_in, w_out, dpre_t, act_t, grads, x_sem, g_sem, w_sem, out_sem = refs[
        2 * chunks + 3 :
    ]
    col = col_ref[0]

    def place(k):
        c = (col & 4) ^ (4 * (k >> 2)) | ((col + k) & 3)
        return pl.multiple_of(c * part, part)

    w_copies, x_copies, g_copies = [], [], []
    blocks = half // part
    for c in range(chunks):
        for q in range(blocks):
            w_copies.append(
                pltpu.make_async_copy(
                    weights.at[c, pl.ds(q * part, part)],
                    w_in.at[pl.ds(c * part, part), pl.ds(q * part, part)],
                    w_sem.at[c * (blocks + 1) + q],
                )
            )
        w_copies.append(
            pltpu.make_async_copy(
                weights.at[c, pl.ds(half, half)],
                w_out.at[:, pl.ds(c * part, part)],
                w_sem.at[c * (blocks + 1) + blocks],
            )
        )
    for side, group in enumerate((own, sib)):
        for k in range(chunks):
            rows, cols = pl.ds(side * tokens, tokens), pl.ds(place(k), part)
            slot = side * chunks + k
            x_copies.append(
                pltpu.make_async_copy(
                    group[k].at[:, pl.ds(0, part)], x_all.at[rows, cols], x_sem.at[slot]
                )
            )
            g_copies.append(
                pltpu.make_async_copy(
                    group[k].at[:, pl.ds(part, part)], g_all.at[rows, cols], g_sem.at[slot]
                )
            )
    for copy in w_copies + x_copies + g_copies:
        copy.start()
    for copy in w_copies + x_copies + g_copies:
        copy.wait()

    step = 256
    for t in range(2 * tokens // step):
        rows = pl.ds(t * step, step)
        pre = jnp.dot(x_all[rows, :], w_in[...], preferred_element_type=jnp.float32)
        back = lax.dot_general(
            g_all[rows, :], w_out[...], (((1,), (1,)), ((), ())), preferred_element_type=jnp.float32
        )
        square = pre * pre
        bend = jnp.tanh(ROOT_2_PI * pre * (1.0 + CUBIC * square))
        act = 0.5 * pre * (1.0 + bend)
        slope = 0.5 * (1.0 + bend) + 0.5 * pre * (1.0 - bend * bend) * (
            ROOT_2_PI * (1.0 + 3.0 * CUBIC * square)
        )
        dpre = (back * slope).astype(jnp.bfloat16)
        dpre_ref[rows, :] = dpre
        dpre_t[:, rows] = dpre.T
        act_t[:, rows] = act.astype(jnp.bfloat16).T

    out_copies = []
    for c in range(chunks):
        cols = pl.ds(c * part, part)
        grads[c, pl.ds(0, half), :] = jnp.dot(
            dpre_t[...], x_all[:, cols], preferred_element_type=jnp.float32
        ).astype(jnp.bfloat16)
        grads[c, pl.ds(half, half), :] = jnp.dot(
            act_t[...], g_all[:, cols], preferred_element_type=jnp.float32
        ).astype(jnp.bfloat16)
        copy = pltpu.make_async_copy(grads.at[c], grads_ref.at[c], out_sem.at[c])
        copy.start()
        out_copies.append(copy)
    for copy in out_copies:
        copy.wait()


def forward(col, own, sib, weights):
    chunks = len(own)
    tokens, part = own[0].shape[0], own[0].shape[1] // 2
    half = weights.shape[1] // 2
    width = chunks * part
    blocks = half // part
    any_space = pl.BlockSpec(memory_space=pl.ANY)
    return pl.pallas_call(
        functools.partial(forward_kernel, chunks=chunks, tokens=tokens, part=part, half=half),
        out_shape=(
            jax.ShapeDtypeStruct((2 * tokens, half), jnp.bfloat16),
            jax.ShapeDtypeStruct((chunks, 2 * half, part), jnp.bfloat16),
        ),
        in_specs=[pl.BlockSpec(memory_space=pltpu.SMEM)] + [any_space] * (2 * chunks + 1),
        out_specs=(pl.BlockSpec(memory_space=pltpu.VMEM), any_space),
        scratch_shapes=[
            pltpu.VMEM((2 * tokens, width), jnp.bfloat16),
            pltpu.VMEM((2 * tokens, width), jnp.bfloat16),
            pltpu.VMEM((width, half), jnp.bfloat16),
            pltpu.VMEM((half, width), jnp.bfloat16),
            pltpu.VMEM((half, 2 * tokens), jnp.bfloat16),
            pltpu.VMEM((half, 2 * tokens), jnp.bfloat16),
            pltpu.VMEM((chunks, 2 * half, part), jnp.bfloat16),
            pltpu.SemaphoreType.DMA((2 * chunks,)),
            pltpu.SemaphoreType.DMA((2 * chunks,)),
            pltpu.SemaphoreType.DMA((chunks * (blocks + 1),)),
            pltpu.SemaphoreType.DMA((chunks,)),
        ],
        compiler_params=pltpu.CompilerParams(vmem_limit_bytes=VMEM_LIMIT),
        cost_estimate=pl.CostEstimate(
            flops=16 * tokens * width * half,
            bytes_accessed=8 * tokens * width + 8 * half * width,
            transcendentals=2 * tokens * half,
        ),
    )(col, *own, *sib, weights)


def input_kernel(col_ref, dpre, weights, out_ref, w_in, sem, *, chunks, part, half):
    col = col_ref[0]
    copies = []
    blocks = half // part
    for k in range(chunks):
        c = (col & 4) ^ (4 * (k >> 2)) | ((col + k) & 3)
        for q in range(blocks):
            copies.append(
                pltpu.make_async_copy(
                    weights.at[c, pl.ds(q * part, part)],
                    w_in.at[pl.ds(k * part, part), pl.ds(q * part, part)],
                    sem.at[k * blocks + q],
                )
            )
    for copy in copies:
        copy.start()
    for copy in copies:
        copy.wait()
    for k in range(chunks):
        where = pl.ds((k >> 2) * part, part)
        out_ref[k & 3, :, where] = lax.dot_general(
            dpre[...],
            w_in[pl.ds(k * part, part), :],
            (((1,), (1,)), ((), ())),
            preferred_element_type=jnp.float32,
        ).astype(jnp.bfloat16)


def input_grad(col, dpre, weights):
    chunks, part = weights.shape[0], weights.shape[2]
    half = weights.shape[1] // 2
    rows = dpre.shape[0]
    blocks = half // part
    return pl.pallas_call(
        functools.partial(input_kernel, chunks=chunks, part=part, half=half),
        out_shape=jax.ShapeDtypeStruct((4, rows, 2 * part), jnp.bfloat16),
        in_specs=[
            pl.BlockSpec(memory_space=pltpu.SMEM),
            pl.BlockSpec(memory_space=pltpu.VMEM),
            pl.BlockSpec(memory_space=pl.ANY),
        ],
        out_specs=pl.BlockSpec(memory_space=pltpu.VMEM),
        scratch_shapes=[
            pltpu.VMEM((chunks * part, half), jnp.bfloat16),
            pltpu.SemaphoreType.DMA((chunks * blocks,)),
        ],
        compiler_params=pltpu.CompilerParams(vmem_limit_bytes=VMEM_LIMIT),
        cost_estimate=pl.CostEstimate(
            flops=2 * rows * chunks * part * half,
            bytes_accessed=2 * rows * (half + chunks * part) + 2 * chunks * part * half,
            transcendentals=0,
        ),
    )(col, dpre, weights)


def on_device(activations, weight_in, weight_out, upstream):
    tokens, part = activations.shape
    half = weight_in.shape[1] // 2
    core = lax.axis_index("depth") % 2
    col = lax.axis_index("col").astype(jnp.int32).reshape(1)

    w_in_here = lax.dynamic_slice(weight_in, (0, core * half), (part, half))
    w_out_here = lax.dynamic_slice(weight_out, (core * half, 0), (half, part))
    packed = jnp.concatenate(
        [w_in_here[:, q * part : (q + 1) * part] for q in range(half // part)] + [w_out_here], axis=0
    )
    weights = lax.all_gather(packed, "row", axis=0, tiled=False)

    mine = jnp.concatenate([activations, upstream], axis=1)
    other = lax.ppermute(mine, "col", Y_LO)
    own = []
    for start in (mine, other):
        own += [start] + [lax.ppermute(start, "col", along_x(-k)) for k in (1, 2, 3)]
    sib = [lax.ppermute(chunk, "depth", CORE) for chunk in own]

    dpre, grads = forward(col, own, sib, weights)

    shares = lax.psum_scatter(grads, "row", scatter_dimension=0, tiled=False)
    summed = (
        shares.astype(jnp.float32) + lax.ppermute(shares, "depth", Y_HI).astype(jnp.float32)
    ).astype(jnp.bfloat16)
    swapped = lax.ppermute(summed, "depth", CORE)
    first = jnp.where(core == 0, summed, swapped).astype(jnp.float32)
    second = jnp.where(core == 0, swapped, summed).astype(jnp.float32)
    grad_weight_in = jnp.concatenate([first[:half].T, second[:half].T], axis=1)
    grad_weight_out = jnp.concatenate([first[half:], second[half:]], axis=0)

    partial = input_grad(col, dpre, weights)
    joined = partial[:, :tokens].astype(jnp.float32) + lax.ppermute(
        partial[:, tokens:], "depth", CORE
    ).astype(jnp.float32)
    joined = joined.astype(jnp.bfloat16)
    total = joined[0].astype(jnp.float32)
    for k in (1, 2, 3):
        total = total + lax.ppermute(joined[k], "col", along_x(k)).astype(jnp.float32)
    passed = lax.ppermute(total[:, part:].astype(jnp.bfloat16), "col", Y_LO)
    grad_input = (total[:, :part] + passed.astype(jnp.float32)).astype(jnp.bfloat16)
    return (grad_input, grad_weight_in, grad_weight_out)


def solution(mesh):
    return jax.shard_map(
        on_device,
        mesh=mesh,
        in_specs=(
            P(("depth", "row"), "col"),
            P("row", "col"),
            P("col", "row"),
            P(("depth", "row"), "col"),
        ),
        out_specs=(P(("depth", "row"), "col"), P("row", "col"), P("col", "row")),
        check_vma=False,
    )
```

```python
import functools

import jax
import jax.numpy as jnp
from jax import lax
from jax.experimental import pallas as pl
from jax.experimental.pallas import tpu as pltpu
from jax.sharding import PartitionSpec as P

VMEM_LIMIT = 48 * 1024 * 1024
ROOT_2_PI = 0.7978845608028654
CUBIC = 0.044715
RELS = (0, 1, -1, 2, -2, 3, -3, 4)

CORE = [(d, d ^ 1) for d in range(4)]
Y_HI = [(d, d ^ 2) for d in range(4)]
Y_LO = [(c, c ^ 4) for c in range(8)]


def along_x(step):
    return [(c, (c & 4) | ((c + step) & 3)) for c in range(8)]


def along_z(step):
    return [(z, (z + step) % 8) for z in range(8)]


def first_core(pairs):
    return [(d * 8 + a, d * 8 + b) for d in (0, 2) for a, b in pairs]


def any_space():
    return pl.BlockSpec(memory_space=pl.ANY)


def vmem():
    return pl.BlockSpec(memory_space=pltpu.VMEM)


def smem():
    return pl.BlockSpec(memory_space=pltpu.SMEM)


def run(copies):
    for copy in copies:
        copy.start()
    for copy in copies:
        copy.wait()


def chunk_of(z, rel, size):
    return pl.multiple_of(((z + rel) & 7) * size, size)


def column_of(col, k, size):
    return pl.multiple_of(((col & 4) ^ (4 * (k >> 2)) | ((col + k) & 3)) * size, size)


def product(place, weight_rows, tokens, payload_ref, slope_ref):
    step = 256
    core = place[2]
    for t in range(tokens.shape[0] // step):
        cols = pl.ds(t * step, step)
        value = lax.dot_general(
            weight_rows[...], tokens[cols, :], (((1,), (1,)), ((), ())), preferred_element_type=jnp.float32
        )

        @pl.when(core == 0)
        def _():
            square = value * value
            bend = jnp.tanh(ROOT_2_PI * value * (1.0 + CUBIC * square))
            payload_ref[:, cols] = (0.5 * value * (1.0 + bend)).astype(jnp.bfloat16)
            slope = 0.5 * (1.0 + bend) + 0.5 * value * (1.0 - bend * bend) * (
                ROOT_2_PI * (1.0 + 3.0 * CUBIC * square)
            )
            slope_ref[:, cols] = slope.astype(jnp.bfloat16)

        @pl.when(core != 0)
        def _():
            payload_ref[:, cols] = value.astype(jnp.bfloat16)
            slope_ref[:, cols] = jnp.ones_like(value).astype(jnp.bfloat16)


def forward_kernel(place, *refs, from_pieces):
    z, col = place[0], place[1]
    pieces = refs[:8]
    if from_pieces:
        tokens_in, outs = refs[8:24], refs[24:]
        payload_ref, slope_ref, cat_ref, weight_rows, tokens, w_sem, t_sem, out_sem = outs
    else:
        cat, payload_ref, slope_ref, weight_rows, tokens, w_sem, t_sem = refs[8:]
    part = pieces[0].shape[1]
    copies = [
        pltpu.make_async_copy(
            pieces[i], weight_rows.at[:, pl.ds(chunk_of(z, rel, part), part)], w_sem.at[i]
        )
        for i, rel in enumerate(RELS)
    ]
    if from_pieces:
        rows = tokens_in[0].shape[0]
        for i in range(16):
            side, k = i // 8, i % 8
            copies.append(
                pltpu.make_async_copy(
                    tokens_in[i],
                    tokens.at[pl.ds(side * rows, rows), pl.ds(column_of(col, k, part), part)],
                    t_sem.at[i],
                )
            )
    else:
        copies.append(pltpu.make_async_copy(cat, tokens, t_sem.at[0]))
    run(copies)
    if from_pieces:
        out = pltpu.make_async_copy(tokens, cat_ref, out_sem)
        out.start()
    product(place, weight_rows, tokens, payload_ref, slope_ref)
    if from_pieces:
        out.wait()


def forward(place, pieces, tokens):
    half, part = pieces[0].shape
    from_pieces = isinstance(tokens, (list, tuple))
    count = 2 * tokens[0].shape[0] if from_pieces else tokens.shape[0]
    width = 8 * part
    out_shape = [jax.ShapeDtypeStruct((half, count), jnp.bfloat16)] * 2
    out_specs = [vmem(), vmem()]
    scratch = [
        pltpu.VMEM((half, width), jnp.bfloat16),
        pltpu.VMEM((count, width), jnp.bfloat16),
        pltpu.SemaphoreType.DMA((8,)),
        pltpu.SemaphoreType.DMA((16,)),
    ]
    if from_pieces:
        out_shape.append(jax.ShapeDtypeStruct((count, width), jnp.bfloat16))
        out_specs.append(any_space())
        scratch.append(pltpu.SemaphoreType.DMA)
    operands = tuple(pieces) + (tuple(tokens) if from_pieces else (tokens,))
    return pl.pallas_call(
        functools.partial(forward_kernel, from_pieces=from_pieces),
        out_shape=out_shape,
        in_specs=[smem()] + [any_space()] * len(operands),
        out_specs=out_specs,
        scratch_shapes=scratch,
        compiler_params=pltpu.CompilerParams(vmem_limit_bytes=VMEM_LIMIT),
        cost_estimate=pl.CostEstimate(
            flops=2 * count * width * half, bytes_accessed=2 * (count + half) * width, transcendentals=count * half
        ),
    )(place, *operands)


def join_kernel(place, recv, slope, joined_ref, *, tokens):
    core = place[2]
    for here, there in ((0, tokens), (tokens, 0)):
        mine, other = pl.ds(here, tokens), pl.ds(there, tokens)

        @pl.when(core == 0)
        def _():
            joined_ref[:, mine] = (
                recv[:, other].astype(jnp.float32) * slope[:, mine].astype(jnp.float32)
            ).astype(jnp.bfloat16)

        @pl.when(core != 0)
        def _():
            joined_ref[:, mine] = recv[:, other]


def join(place, recv, slope):
    half, count = recv.shape
    return pl.pallas_call(
        functools.partial(join_kernel, tokens=count // 2),
        out_shape=jax.ShapeDtypeStruct((half, count), jnp.bfloat16),
        in_specs=[smem(), vmem(), vmem()],
        out_specs=vmem(),
        compiler_params=pltpu.CompilerParams(vmem_limit_bytes=VMEM_LIMIT),
        cost_estimate=pl.CostEstimate(
            flops=half * count, bytes_accessed=6 * half * count, transcendentals=0
        ),
    )(place, recv, slope)


def weight_kernel(place, joined, cat, *refs, rels, part):
    outs, (tokens, sem) = refs[: len(rels)], refs[len(rels) :]
    copies = [
        pltpu.make_async_copy(
            cat.at[:, pl.ds(chunk_of(place[0], rel, part), part)], tokens.at[i], sem.at[i]
        )
        for i, rel in enumerate(rels)
    ]
    for copy in copies:
        copy.start()
    for i, copy in enumerate(copies):
        copy.wait()
        outs[i][...] = jnp.dot(joined[...], tokens[i], preferred_element_type=jnp.float32).astype(
            jnp.bfloat16
        )


def weight_terms(place, joined, cat, rels):
    half, count = joined.shape
    part = cat.shape[1] // 8
    return pl.pallas_call(
        functools.partial(weight_kernel, rels=rels, part=part),
        out_shape=[jax.ShapeDtypeStruct((half, part), jnp.bfloat16)] * len(rels),
        in_specs=[smem(), vmem(), any_space()],
        out_specs=[vmem()] * len(rels),
        scratch_shapes=[
            pltpu.VMEM((len(rels), count, part), jnp.bfloat16),
            pltpu.SemaphoreType.DMA((len(rels),)),
        ],
        compiler_params=pltpu.CompilerParams(vmem_limit_bytes=VMEM_LIMIT),
        cost_estimate=pl.CostEstimate(
            flops=2 * half * count * part * len(rels),
            bytes_accessed=2 * half * count + 2 * (half + count) * part * len(rels),
            transcendentals=0,
        ),
    )(place, joined, cat)


def input_kernel(place, first, second, *refs, steps, part):
    pieces, (out_ref, weight_rows, sem) = refs[:16], refs[16:]
    z, col = place[0], place[1]
    half = first.shape[0]
    run(
        [
            pltpu.make_async_copy(
                pieces[8 * f + i],
                weight_rows.at[pl.ds(f * half, half), pl.ds(chunk_of(z, rel, part), part)],
                sem.at[8 * f + i],
            )
            for f in range(2)
            for i, rel in enumerate(RELS)
        ]
    )
    for n, step in enumerate(steps):
        for k in (step, step + 4):
            cols = pl.ds(column_of(col, k, part), part)
            total = None
            for f, joined in enumerate((first, second)):
                term = lax.dot_general(
                    joined[...],
                    weight_rows[pl.ds(f * half, half), cols],
                    (((0,), (0,)), ((), ())),
                    preferred_element_type=jnp.float32,
                )
                total = term if total is None else total + term
            out_ref[n, :, pl.ds((k >> 2) * part, part)] = total.astype(jnp.bfloat16)


def input_terms(place, first, second, pieces, steps):
    half, count = first.shape
    part = pieces[0].shape[1]
    return pl.pallas_call(
        functools.partial(input_kernel, steps=steps, part=part),
        out_shape=jax.ShapeDtypeStruct((len(steps), count, 2 * part), jnp.bfloat16),
        in_specs=[smem(), vmem(), vmem()] + [any_space()] * 16,
        out_specs=vmem(),
        scratch_shapes=[
            pltpu.VMEM((2 * half, 8 * part), jnp.bfloat16),
            pltpu.SemaphoreType.DMA((16,)),
        ],
        compiler_params=pltpu.CompilerParams(vmem_limit_bytes=VMEM_LIMIT),
        cost_estimate=pl.CostEstimate(
            flops=8 * half * count * part * len(steps),
            bytes_accessed=4 * half * (count + 8 * part) + 4 * count * part * len(steps),
            transcendentals=0,
        ),
    )(place, first, second, *pieces)


def gather_z(piece, last_step):
    above, below = [piece], [piece]
    for _ in range(3):
        above.append(lax.ppermute(above[-1], "row", along_z(-1)))
        below.append(lax.ppermute(below[-1], "row", along_z(1)))
    far = lax.ppermute((above if last_step < 0 else below)[-1], "row", along_z(last_step))
    return [piece, above[1], below[1], above[2], below[2], above[3], below[3], far]


def gather_x(piece, last_step):
    above = lax.ppermute(piece, "col", along_x(-1))
    below = lax.ppermute(piece, "col", along_x(1))
    far = lax.ppermute(above if last_step < 0 else below, "col", along_x(last_step))
    return [piece, above, far, below]


def add(*terms):
    total = terms[0].astype(jnp.float32)
    for term in terms[1:]:
        total = total + term.astype(jnp.float32)
    return total


def scatter_z(terms, last_step):
    far = lax.ppermute(terms[4], "row", along_z(-last_step))
    up, down = terms[3], terms[-3]
    if last_step < 0:
        up = add(up, far).astype(jnp.bfloat16)
    else:
        down = add(down, far).astype(jnp.bfloat16)
    for rel in (2, 1):
        up = add(terms[rel], lax.ppermute(up, "row", along_z(1))).astype(jnp.bfloat16)
        down = add(terms[-rel], lax.ppermute(down, "row", along_z(-1))).astype(jnp.bfloat16)
    up = lax.ppermute(up, "row", along_z(1))
    down = lax.ppermute(down, "row", along_z(-1))
    return add(terms[0], up, down).astype(jnp.bfloat16)


def on_device(activations, weight_in, weight_out, upstream):
    tokens, part = activations.shape
    half = weight_in.shape[1] // 2
    core = lax.axis_index("depth") % 2
    first = core == 0
    place = jnp.stack([lax.axis_index("row"), lax.axis_index("col"), core]).astype(jnp.int32)

    weight = jnp.where(first, weight_in.T, weight_out)
    mine = jnp.where(first, activations, upstream)
    other = lax.ppermute(jnp.where(first, upstream, activations), "depth", CORE)
    halves = [gather_z(weight[:half], -1), gather_z(weight[half:], 1)]
    pieces = []
    for piece, step in ((mine, -1), (other, 1)):
        pieces += gather_x(piece, step) + gather_x(lax.ppermute(piece, "col", Y_LO), step)

    payload, slope, cat = forward(place, halves[0], pieces)
    second_payload, second_slope = forward(place, halves[1], cat)
    joined = [
        join(place, lax.ppermute(payload, "depth", CORE), slope),
        join(place, lax.ppermute(second_payload, "depth", CORE), second_slope),
    ]

    sums = []
    for hidden, step in zip(joined, (-1, 1)):
        terms = {}
        for rels in ((4,), (3, -3), (2, -2), (1, -1, 0)):
            terms.update(zip(rels, weight_terms(place, hidden, cat, rels)))
        share = scatter_z(terms, step)
        share = add(share, lax.ppermute(share, "depth", Y_HI)).astype(jnp.bfloat16)
        swapped = lax.ppermute(share, "depth", CORE)
        sums.append((share, swapped))
    grad_weight_in = jnp.concatenate(
        [jnp.where(first, share, swapped).astype(jnp.float32).T for share, swapped in sums], axis=1
    )
    grad_weight_out = jnp.concatenate(
        [jnp.where(first, swapped, share).astype(jnp.float32) for share, swapped in sums], axis=0
    )

    flat = halves[0] + halves[1]
    total = None
    for step in (2, 1, 3, 0):
        term = input_terms(place, joined[0], joined[1], flat, (step,))[0]
        if step:
            term = lax.ppermute(term, ("depth", "col"), first_core(along_x(step)))
        total = term.astype(jnp.float32) if total is None else total + term.astype(jnp.float32)
    passed = lax.ppermute(total[:, part:].astype(jnp.bfloat16), ("depth", "col"), first_core(Y_LO))
    total = add(total[:, :part], passed).astype(jnp.bfloat16)
    theirs = lax.ppermute(total[tokens:], "depth", [(0, 1), (2, 3)])
    grad_input = jnp.where(first, total[:tokens], theirs)
    return (grad_input, grad_weight_in, grad_weight_out)


def solution(mesh):
    return jax.shard_map(
        on_device,
        mesh=mesh,
        in_specs=(
            P(("depth", "row"), "col"),
            P("row", "col"),
            P("col", "row"),
            P(("depth", "row"), "col"),
        ),
        out_specs=(P(("depth", "row"), "col"), P("row", "col"), P("col", "row")),
        check_vma=False,
    )
```

```python
import functools

import jax
import jax.numpy as jnp
from jax import lax
from jax.experimental import pallas as pl
from jax.experimental.pallas import tpu as pltpu
from jax.sharding import PartitionSpec as P

VMEM_LIMIT = 60 * 1024 * 1024
ROOT_2_PI = 0.7978845608028654
CUBIC = 0.044715

CORE = [(d, d ^ 1) for d in range(4)]
Y_HI = [(d, d ^ 2) for d in range(4)]
Y_LO = [(c, c ^ 4) for c in range(8)]


def along_x(step):
    return [(c, (c & 4) | ((c + step) & 3)) for c in range(8)]


def along_z(step):
    return [(z, (z + step) % 8) for z in range(8)]


def by_core(first, second):
    return [
        (d * 8 + a, d * 8 + b) for d in range(4) for a, b in (first if d % 2 == 0 else second)
    ]


def after(value, *others):
    return lax.optimization_barrier((value, *others))[0]


def hbm():
    return pl.BlockSpec(memory_space=pl.ANY)


def vmem():
    return pl.BlockSpec(memory_space=pltpu.VMEM)


def smem():
    return pl.BlockSpec(memory_space=pltpu.SMEM)


def chunk_of(z, rel, size):
    return pl.multiple_of(((z + rel) & 7) * size, size)


def column_of(col, k, size):
    return pl.multiple_of(((col & 4) ^ (4 * (k >> 2)) | ((col + k) & 3)) * size, size)


def pack_kernel(place, activations, upstream, weight_in, weight_out, mine, packed):
    part = activations.shape[1]
    half = packed.shape[0] // 2
    at = pl.multiple_of(place[2] * half, half)
    for q in range(half // part):
        packed[pl.ds(q * part, part), :] = weight_in[:, pl.ds(pl.multiple_of(at + q * part, part), part)]
    packed[pl.ds(half, half), :] = weight_out[pl.ds(at, half), :]
    mine[:, pl.ds(0, part)] = activations[...]
    mine[:, pl.ds(part, part)] = upstream[...]


def pack(place, activations, upstream, weight_in, weight_out):
    tokens, part = activations.shape
    half = weight_in.shape[1] // 2
    return pl.pallas_call(
        pack_kernel,
        out_shape=(
            jax.ShapeDtypeStruct((tokens, 2 * part), jnp.bfloat16),
            jax.ShapeDtypeStruct((2 * half, part), jnp.bfloat16),
        ),
        in_specs=[smem()] + [vmem()] * 4,
        out_specs=(vmem(), vmem()),
        compiler_params=pltpu.CompilerParams(vmem_limit_bytes=VMEM_LIMIT),
    )(place, activations, upstream, weight_in, weight_out)


def token_copies(col, own, sib, x_all, g_all, x_sem, g_sem, tokens, part):
    x_copies, g_copies = ([], []), ([], [])
    for side, group in enumerate((own, sib)):
        for k in range(8):
            rows, cols = pl.ds(side * tokens, tokens), pl.ds(column_of(col, k, part), part)
            slot = side * 8 + k
            x_copies[side].append(
                pltpu.make_async_copy(
                    group[k].at[:, pl.ds(0, part)], x_all.at[rows, cols], x_sem.at[slot]
                )
            )
            g_copies[side].append(
                pltpu.make_async_copy(
                    group[k].at[:, pl.ds(part, part)], g_all.at[rows, cols], g_sem.at[slot]
                )
            )
    return x_copies, g_copies


def w_in_copies(weights, w_in, sem, part, half):
    blocks = half // part
    return [
        pltpu.make_async_copy(
            weights.at[c, pl.ds(q * part, part)],
            w_in.at[pl.ds(c * part, part), pl.ds(q * part, part)],
            sem.at[c * blocks + q],
        )
        for c in range(8)
        for q in range(blocks)
    ]


def start(*groups):
    for group in groups:
        for copy in group:
            copy.start()


def wait(*groups):
    for group in groups:
        for copy in group:
            copy.wait()


TILES = ((0, 384), (384, 256))


def forward_kernel(place, *refs, tokens, part, half):
    own, sib, weights = refs[:8], refs[8:16], refs[16]
    dpre_ref, terms_ref = refs[17:19]
    x_all, g_all, w_in, w_out, both, terms, x_sem, g_sem, w_sem, v_sem, out_sem = refs[19:]
    x_copies, g_copies = token_copies(
        place[1], own, sib, x_all, g_all, x_sem, g_sem, tokens, part
    )
    w_copies = w_in_copies(weights, w_in, w_sem, part, half)
    v_copies = [
        pltpu.make_async_copy(
            weights.at[c, pl.ds(half, half)], w_out.at[:, pl.ds(c * part, part)], v_sem.at[c]
        )
        for c in range(8)
    ]
    start(w_copies, x_copies[0], v_copies, g_copies[0], x_copies[1], g_copies[1])
    wait(w_copies)
    for side in range(2):
        wait(x_copies[side])
        if side:
            wait(g_copies[side])
        for n, (first, size) in enumerate(TILES):
            rows = pl.ds(side * tokens + first, size)
            pre = jnp.dot(x_all[rows, :], w_in[...], preferred_element_type=jnp.float32)
            if side == 0 and n == 0:
                wait(v_copies, g_copies[0])
            back = lax.dot_general(
                g_all[rows, :], w_out[...], (((1,), (1,)), ((), ())), preferred_element_type=jnp.float32
            )
            square = pre * pre
            bend = jnp.tanh(ROOT_2_PI * pre * (1.0 + CUBIC * square))
            act = 0.5 * pre * (1.0 + bend)
            slope = 0.5 * (1.0 + bend) + 0.5 * pre * (1.0 - bend * bend) * (
                ROOT_2_PI * (1.0 + 3.0 * CUBIC * square)
            )
            dpre = (back * slope).astype(jnp.bfloat16)
            dpre_ref[rows, :] = dpre
            both[pl.ds(0, half), rows] = dpre.T
            both[pl.ds(half, half), rows] = act.astype(jnp.bfloat16).T

    outs = []
    for c in range(8):
        cols = pl.ds(c * part, part)
        for n, source in enumerate((x_all, g_all)):
            rows = pl.ds(n * half, half)
            terms[c, rows, :] = jnp.dot(
                both[rows, :], source[:, cols], preferred_element_type=jnp.float32
            ).astype(jnp.bfloat16)
        outs.append(pltpu.make_async_copy(terms.at[c], terms_ref.at[c], out_sem.at[c]))
        outs[-1].start()
    wait(outs)


def forward(place, own, sib, weights):
    tokens, part = own[0].shape[0], own[0].shape[1] // 2
    half = weights.shape[1] // 2
    width = 8 * part
    bf16 = jnp.bfloat16
    return pl.pallas_call(
        functools.partial(forward_kernel, tokens=tokens, part=part, half=half),
        out_shape=[
            jax.ShapeDtypeStruct((2 * tokens, half), bf16),
            jax.ShapeDtypeStruct((8, 2 * half, part), bf16),
        ],
        in_specs=[smem()] + [hbm()] * 17,
        out_specs=[vmem(), hbm()],
        scratch_shapes=[
            pltpu.VMEM((2 * tokens, width), bf16),
            pltpu.VMEM((2 * tokens, width), bf16),
            pltpu.VMEM((width, half), bf16),
            pltpu.VMEM((half, width), bf16),
            pltpu.VMEM((2 * half, 2 * tokens), bf16),
            pltpu.VMEM((8, 2 * half, part), bf16),
            pltpu.SemaphoreType.DMA((16,)),
            pltpu.SemaphoreType.DMA((16,)),
            pltpu.SemaphoreType.DMA((8 * (half // part),)),
            pltpu.SemaphoreType.DMA((8,)),
            pltpu.SemaphoreType.DMA((8,)),
        ],
        compiler_params=pltpu.CompilerParams(vmem_limit_bytes=VMEM_LIMIT),
        cost_estimate=pl.CostEstimate(
            flops=16 * tokens * width * half,
            bytes_accessed=8 * tokens * width + 12 * half * width,
            transcendentals=2 * tokens * half,
        ),
    )(place, *own, *sib, weights)


def input_kernel(place, dpre, weights, sib_ref, own_ref, w_in, sem, *, part, half):
    col = place[1]
    tokens = own_ref.shape[1]
    copies = w_in_copies(weights, w_in, sem, part, half)
    start(copies)
    wait(copies)
    for out_ref, rows in ((sib_ref, pl.ds(tokens, tokens)), (own_ref, pl.ds(0, tokens))):
        for k in range(8):
            out_ref[k & 3, :, pl.ds((k >> 2) * part, part)] = lax.dot_general(
                dpre[rows, :],
                w_in[pl.ds(column_of(col, k, part), part), :],
                (((1,), (1,)), ((), ())),
                preferred_element_type=jnp.float32,
            ).astype(jnp.bfloat16)


def input_terms(place, dpre, weights):
    count, half = dpre.shape
    part = weights.shape[2]
    out = jax.ShapeDtypeStruct((4, count // 2, 2 * part), jnp.bfloat16)
    return pl.pallas_call(
        functools.partial(input_kernel, part=part, half=half),
        out_shape=(out, out),
        in_specs=[smem(), vmem(), hbm()],
        out_specs=(vmem(), vmem()),
        scratch_shapes=[
            pltpu.VMEM((8 * part, half), jnp.bfloat16),
            pltpu.SemaphoreType.DMA((8 * (half // part),)),
        ],
        compiler_params=pltpu.CompilerParams(vmem_limit_bytes=VMEM_LIMIT),
        cost_estimate=pl.CostEstimate(
            flops=16 * half * count * part,
            bytes_accessed=2 * count * half + 16 * (half + count) * part,
            transcendentals=0,
        ),
    )(place, dpre, weights)


def add(*terms):
    total = terms[0].astype(jnp.float32)
    for term in terms[1:]:
        total = total + term.astype(jnp.float32)
    return total


def on_device(activations, weight_in, weight_out, upstream):
    tokens, part = activations.shape
    core = lax.axis_index("depth") % 2
    first = core == 0
    place = jnp.stack([lax.axis_index("row"), lax.axis_index("col"), core]).astype(jnp.int32)
    bf16 = jnp.bfloat16

    def swap(chunk):
        return lax.ppermute(chunk, "depth", CORE)

    def across(up, down):
        return lax.ppermute(
            jnp.where(first, up, down), ("depth", "col"), by_core(along_x(-1), along_x(1))
        )

    mine, packed = pack(place, activations, upstream, weight_in, weight_out)
    weights = lax.all_gather(packed, "row", axis=0, tiled=False)

    own = {0: mine}
    own[1] = lax.ppermute(mine, "col", along_x(-1))
    own[3] = lax.ppermute(mine, "col", along_x(1))
    own[4] = lax.ppermute(mine, "col", Y_LO)
    sib = {0: swap(mine)}
    own[5] = lax.ppermute(own[4], "col", along_x(-1))
    own[7] = lax.ppermute(own[4], "col", along_x(1))
    own[2] = across(after(own[1], own[4]), own[3])
    for k in (1, 3, 4):
        sib[k] = swap(after(own[k], own[1], own[3], own[4]))
    own[6] = across(own[5], own[7])
    for k in (5, 7, 2):
        sib[k] = swap(after(own[k], own[5], own[7]))
    sib[6] = swap(own[6])
    own, sib = [[group[k] for k in range(8)] for group in (own, sib)]

    dpre, terms = forward(place, own, sib, weights)

    shares = lax.psum_scatter(terms, "row", scatter_dimension=0, tiled=False)
    theirs, ours = input_terms(place, dpre, weights)
    joined = add(ours, swap(theirs)).astype(bf16)
    moved = [lax.ppermute(joined[k], "col", along_x(k)) for k in (2, 1, 3)]
    total = add(joined[0], *moved)
    passed = lax.ppermute(total[:, part:].astype(bf16), "col", Y_LO)
    grad_input = add(total[:, :part], passed).astype(bf16)

    shares = after(shares, grad_input)
    shares = add(shares, lax.ppermute(shares, "depth", Y_HI)).astype(bf16)
    swapped = swap(shares)
    left = jnp.where(first, shares, swapped).astype(jnp.float32)
    right = jnp.where(first, swapped, shares).astype(jnp.float32)
    half = shares.shape[0] // 2
    grad_weight_in = jnp.concatenate([left[:half].T, right[:half].T], axis=1)
    grad_weight_out = jnp.concatenate([left[half:], right[half:]], axis=0)
    return (grad_input, grad_weight_in, grad_weight_out)


def solution(mesh):
    return jax.shard_map(
        on_device,
        mesh=mesh,
        in_specs=(
            P(("depth", "row"), "col"),
            P("row", "col"),
            P("col", "row"),
            P(("depth", "row"), "col"),
        ),
        out_specs=(P(("depth", "row"), "col"), P("row", "col"), P("col", "row")),
        check_vma=False,
    )
```

```python
import functools

import jax
import jax.numpy as jnp
from jax import lax
from jax.experimental import pallas as pl
from jax.experimental.pallas import tpu as pltpu
from jax.sharding import PartitionSpec as P

VMEM_LIMIT = 60 * 1024 * 1024
ROOT_2_PI = 0.7978845608028654
CUBIC = 0.044715

CORE = [(d, d ^ 1) for d in range(4)]
Y_HI = [(d, d ^ 2) for d in range(4)]
Y_LO = [(c, c ^ 4) for c in range(8)]


def along_x(step):
    return [(c, (c & 4) | ((c + step) & 3)) for c in range(8)]


def along_z(step):
    return [(z, (z + step) % 8) for z in range(8)]


def by_core(first, second):
    return [
        (d * 8 + a, d * 8 + b) for d in range(4) for a, b in (first if d % 2 == 0 else second)
    ]


def after(value, *others):
    return lax.optimization_barrier((value, *others))[0]


def hbm():
    return pl.BlockSpec(memory_space=pl.ANY)


def vmem():
    return pl.BlockSpec(memory_space=pltpu.VMEM)


def smem():
    return pl.BlockSpec(memory_space=pltpu.SMEM)


def chunk_of(z, rel, size):
    return pl.multiple_of(((z + rel) & 7) * size, size)


def column_of(col, k, size):
    return pl.multiple_of(((col & 4) ^ (4 * (k >> 2)) | ((col + k) & 3)) * size, size)


def pack_kernel(place, activations, upstream, weight_in, weight_out, mine, packed):
    part = activations.shape[1]
    half = packed.shape[0] // 2
    at = pl.multiple_of(place[2] * half, half)
    for q in range(half // part):
        packed[pl.ds(q * part, part), :] = weight_in[:, pl.ds(pl.multiple_of(at + q * part, part), part)]
    packed[pl.ds(half, half), :] = weight_out[pl.ds(at, half), :]
    mine[:, pl.ds(0, part)] = activations[...]
    mine[:, pl.ds(part, part)] = upstream[...]


def pack(place, activations, upstream, weight_in, weight_out):
    tokens, part = activations.shape
    half = weight_in.shape[1] // 2
    return pl.pallas_call(
        pack_kernel,
        out_shape=(
            jax.ShapeDtypeStruct((tokens, 2 * part), jnp.bfloat16),
            jax.ShapeDtypeStruct((2 * half, part), jnp.bfloat16),
        ),
        in_specs=[smem()] + [vmem()] * 4,
        out_specs=(vmem(), vmem()),
        compiler_params=pltpu.CompilerParams(vmem_limit_bytes=VMEM_LIMIT),
    )(place, activations, upstream, weight_in, weight_out)


def token_copies(col, own, sib, x_all, g_all, x_sem, g_sem, tokens, part):
    x_copies, g_copies = ([], []), ([], [])
    for side, group in enumerate((own, sib)):
        for k in range(8):
            rows, cols = pl.ds(side * tokens, tokens), pl.ds(column_of(col, k, part), part)
            slot = side * 8 + k
            x_copies[side].append(
                pltpu.make_async_copy(
                    group[k].at[:, pl.ds(0, part)], x_all.at[rows, cols], x_sem.at[slot]
                )
            )
            g_copies[side].append(
                pltpu.make_async_copy(
                    group[k].at[:, pl.ds(part, part)], g_all.at[rows, cols], g_sem.at[slot]
                )
            )
    return x_copies, g_copies


def w_in_copies(weights, w_in, sem, part, half):
    blocks = half // part
    return [
        pltpu.make_async_copy(
            weights.at[c, pl.ds(q * part, part)],
            w_in.at[pl.ds(c * part, part), pl.ds(q * part, part)],
            sem.at[c * blocks + q],
        )
        for c in range(8)
        for q in range(blocks)
    ]


def start(*groups):
    for group in groups:
        for copy in group:
            copy.start()


def wait(*groups):
    for group in groups:
        for copy in group:
            copy.wait()


TILES = ((0, 384), (384, 256), (640, 384), (1024, 256))


def forward_kernel(place, *refs, tokens, part, half):
    own, sib, weights = refs[:8], refs[8:16], refs[16]
    dpre_ref, terms_ref = refs[17:19]
    x_all, g_all, w_in, w_out, both, terms, x_sem, g_sem, w_sem, v_sem, out_sem = refs[19:]
    x_copies, g_copies = token_copies(
        place[1], own, sib, x_all, g_all, x_sem, g_sem, tokens, part
    )
    w_copies = w_in_copies(weights, w_in, w_sem, part, half)
    v_copies = [
        pltpu.make_async_copy(
            weights.at[c, pl.ds(half, half)], w_out.at[:, pl.ds(c * part, part)], v_sem.at[c]
        )
        for c in range(8)
    ]
    start(w_copies, x_copies[0])
    wait(w_copies, x_copies[0])
    start(v_copies, g_copies[0])
    for side in range(2):
        rows = pl.ds(side * tokens, tokens)
        if side:
            wait(x_copies[1])
        pre = jnp.dot(x_all[rows, :], w_in[...], preferred_element_type=jnp.float32)
        if side == 0:
            start(x_copies[1])
            wait(v_copies, g_copies[0])
            start(g_copies[1])
        else:
            wait(g_copies[1])
        back = lax.dot_general(
            g_all[rows, :], w_out[...], (((1,), (1,)), ((), ())), preferred_element_type=jnp.float32
        )
        square = pre * pre
        weight = 0.5 + 0.5 * jnp.tanh(pre * (ROOT_2_PI + (ROOT_2_PI * CUBIC) * square))
        act = pre * weight
        slope = weight + act * (1.0 - weight) * (
            2.0 * ROOT_2_PI + (6.0 * ROOT_2_PI * CUBIC) * square
        )
        dpre = (back * slope).astype(jnp.bfloat16)
        dpre_ref[rows, :] = dpre
        both[pl.ds(0, half), rows] = dpre.T
        both[pl.ds(half, half), rows] = act.astype(jnp.bfloat16).T

    outs = []
    for c in range(8):
        cols = pl.ds(c * part, part)
        for n, source in enumerate((x_all, g_all)):
            rows = pl.ds(n * half, half)
            terms[c, rows, :] = jnp.dot(
                both[rows, :], source[:, cols], preferred_element_type=jnp.float32
            ).astype(jnp.bfloat16)
        outs.append(pltpu.make_async_copy(terms.at[c], terms_ref.at[c], out_sem.at[c]))
        outs[-1].start()
    wait(outs)


def forward(place, own, sib, weights):
    tokens, part = own[0].shape[0], own[0].shape[1] // 2
    half = weights.shape[1] // 2
    width = 8 * part
    bf16 = jnp.bfloat16
    return pl.pallas_call(
        functools.partial(forward_kernel, tokens=tokens, part=part, half=half),
        out_shape=[
            pltpu.VMEM((2 * tokens, half), bf16),
            pltpu.HBM((8, 2 * half, part), bf16),
        ],
        in_specs=[smem()] + [hbm()] * 17,
        out_specs=[vmem(), hbm()],
        scratch_shapes=[
            pltpu.VMEM((2 * tokens, width), bf16),
            pltpu.VMEM((2 * tokens, width), bf16),
            pltpu.VMEM((width, half), bf16),
            pltpu.VMEM((half, width), bf16),
            pltpu.VMEM((2 * half, 2 * tokens), bf16),
            pltpu.VMEM((8, 2 * half, part), bf16),
            pltpu.SemaphoreType.DMA((16,)),
            pltpu.SemaphoreType.DMA((16,)),
            pltpu.SemaphoreType.DMA((8 * (half // part),)),
            pltpu.SemaphoreType.DMA((8,)),
            pltpu.SemaphoreType.DMA((8,)),
        ],
        compiler_params=pltpu.CompilerParams(vmem_limit_bytes=VMEM_LIMIT),
        cost_estimate=pl.CostEstimate(
            flops=16 * tokens * width * half,
            bytes_accessed=8 * tokens * width + 12 * half * width,
            transcendentals=2 * tokens * half,
        ),
    )(place, *own, *sib, pltpu.with_memory_space_constraint(weights, pltpu.HBM))


def input_kernel(place, dpre, weights, out_ref, w_in, sem, *, side, part, half):
    col = place[1]
    tokens = out_ref.shape[1]
    copies = w_in_copies(weights, w_in, sem, part, half)
    start(copies)
    wait(copies)
    for k in range(8):
        out_ref[k & 3, :, pl.ds((k >> 2) * part, part)] = lax.dot_general(
            dpre[pl.ds(side * tokens, tokens), :],
            w_in[pl.ds(column_of(col, k, part), part), :],
            (((1,), (1,)), ((), ())),
            preferred_element_type=jnp.float32,
        ).astype(jnp.bfloat16)


def input_terms(place, dpre, weights, side):
    tokens, half = dpre.shape[0] // 2, dpre.shape[1]
    part = weights.shape[2]
    return pl.pallas_call(
        functools.partial(input_kernel, side=side, part=part, half=half),
        out_shape=jax.ShapeDtypeStruct((4, tokens, 2 * part), jnp.bfloat16),
        in_specs=[smem(), vmem(), hbm()],
        out_specs=vmem(),
        scratch_shapes=[
            pltpu.VMEM((8 * part, half), jnp.bfloat16),
            pltpu.SemaphoreType.DMA((8 * (half // part),)),
        ],
        compiler_params=pltpu.CompilerParams(vmem_limit_bytes=24 * 1024 * 1024),
        cost_estimate=pl.CostEstimate(
            flops=16 * half * tokens * part,
            bytes_accessed=2 * tokens * half + 16 * (half + tokens) * part,
            transcendentals=0,
        ),
    )(
        place,
        pltpu.with_memory_space_constraint(dpre, pltpu.VMEM),
        pltpu.with_memory_space_constraint(weights, pltpu.HBM),
    )


def add(*terms):
    total = terms[0].astype(jnp.float32)
    for term in terms[1:]:
        total = total + term.astype(jnp.float32)
    return total


def on_device(activations, weight_in, weight_out, upstream):
    tokens, part = activations.shape
    core = lax.axis_index("depth") % 2
    first = core == 0
    place = jnp.stack([lax.axis_index("row"), lax.axis_index("col"), core]).astype(jnp.int32)
    bf16 = jnp.bfloat16

    def swap(chunk):
        return lax.ppermute(chunk, "depth", CORE)

    def across(up, down):
        return lax.ppermute(
            jnp.where(first, up, down), ("depth", "col"), by_core(along_x(-1), along_x(1))
        )

    mine, packed = pack(place, activations, upstream, weight_in, weight_out)
    weights = lax.all_gather(packed, "row", axis=0, tiled=False)

    own = {0: mine}
    own[1] = lax.ppermute(mine, "col", along_x(-1))
    own[3] = lax.ppermute(mine, "col", along_x(1))
    own[4] = lax.ppermute(mine, "col", Y_LO)
    sib = {0: swap(mine)}
    own[5] = lax.ppermute(own[4], "col", along_x(-1))
    own[7] = lax.ppermute(own[4], "col", along_x(1))
    own[2] = across(after(own[1], own[4]), own[3])
    for k in (1, 3, 4):
        sib[k] = swap(after(own[k], own[1], own[3], own[4]))
    own[6] = across(own[5], own[7])
    for k in (5, 7, 2):
        sib[k] = swap(after(own[k], own[5], own[7]))
    sib[6] = swap(own[6])
    own, sib = [[group[k] for k in range(8)] for group in (own, sib)]

    dpre, terms = forward(place, own, sib, weights)

    shares = lax.psum_scatter(terms, "row", scatter_dimension=0, tiled=False)
    theirs = swap(input_terms(place, dpre, weights, 1))
    joined = add(input_terms(place, dpre, weights, 0), theirs).astype(bf16)
    moved = [lax.ppermute(joined[k], "col", along_x(k)) for k in (2, 1, 3)]
    total = add(joined[0], *moved)
    passed = lax.ppermute(total[:, part:].astype(bf16), "col", Y_LO)
    grad_input = add(total[:, :part], passed).astype(bf16)

    shares = after(shares, grad_input)
    away = lax.ppermute(shares, "depth", Y_HI)
    here, there = add(shares, away), add(swap(shares), swap(away))
    left, right = jnp.where(first, here, there), jnp.where(first, there, here)
    half = shares.shape[0] // 2
    grad_weight_in = jnp.concatenate([left[:half].T, right[:half].T], axis=1)
    grad_weight_out = jnp.concatenate([left[half:], right[half:]], axis=0)
    return (grad_input, grad_weight_in, grad_weight_out)


def solution(mesh):
    return jax.shard_map(
        on_device,
        mesh=mesh,
        in_specs=(
            P(("depth", "row"), "col"),
            P("row", "col"),
            P("col", "row"),
            P(("depth", "row"), "col"),
        ),
        out_specs=(P(("depth", "row"), "col"), P("row", "col"), P("col", "row")),
        check_vma=False,
    )
```

```python
import functools

import jax
import jax.numpy as jnp
from jax import lax
from jax.experimental import pallas as pl
from jax.experimental.pallas import tpu as pltpu
from jax.sharding import PartitionSpec as P

VMEM_LIMIT = 60 * 1024 * 1024
ROOT_2_PI = 0.7978845608028654
CUBIC = 0.044715

CORE = [(d, d ^ 1) for d in range(4)]
Y_HI = [(d, d ^ 2) for d in range(4)]
Y_LO = [(c, c ^ 4) for c in range(8)]


def along_x(step):
    return [(c, (c & 4) | ((c + step) & 3)) for c in range(8)]


def along_z(step):
    return [(z, (z + step) % 8) for z in range(8)]


def by_core(first, second):
    return [
        (d * 8 + a, d * 8 + b) for d in range(4) for a, b in (first if d % 2 == 0 else second)
    ]


def after(value, *others):
    return lax.optimization_barrier((value, *others))[0]


def hbm():
    return pl.BlockSpec(memory_space=pl.ANY)


def vmem():
    return pl.BlockSpec(memory_space=pltpu.VMEM)


def smem():
    return pl.BlockSpec(memory_space=pltpu.SMEM)


def chunk_of(z, rel, size):
    return pl.multiple_of(((z + rel) & 7) * size, size)


def column_of(col, k, size):
    return pl.multiple_of(((col & 4) ^ (4 * (k >> 2)) | ((col + k) & 3)) * size, size)


def weights_kernel(place, weight_in, weight_out, packed):
    part = weight_in.shape[0]
    half = packed.shape[0] // 2
    at = pl.multiple_of(place[2] * half, half)
    for q in range(half // part):
        packed[pl.ds(q * part, part), :] = weight_in[:, pl.ds(pl.multiple_of(at + q * part, part), part)]
    packed[pl.ds(half, half), :] = weight_out[pl.ds(at, half), :]


def pack_weights(place, weight_in, weight_out):
    part, half = weight_in.shape[0], weight_in.shape[1] // 2
    return pl.pallas_call(
        weights_kernel,
        out_shape=jax.ShapeDtypeStruct((2 * half, part), jnp.bfloat16),
        in_specs=[smem(), vmem(), vmem()],
        out_specs=vmem(),
        compiler_params=pltpu.CompilerParams(vmem_limit_bytes=VMEM_LIMIT),
    )(place, weight_in, weight_out)


def tokens_kernel(activations, upstream, mine):
    part = activations.shape[1]
    mine[:, pl.ds(0, part)] = activations[...]
    mine[:, pl.ds(part, part)] = upstream[...]


def pack_tokens(activations, upstream):
    tokens, part = activations.shape
    return pl.pallas_call(
        tokens_kernel,
        out_shape=jax.ShapeDtypeStruct((tokens, 2 * part), jnp.bfloat16),
        in_specs=[vmem(), vmem()],
        out_specs=vmem(),
        compiler_params=pltpu.CompilerParams(vmem_limit_bytes=VMEM_LIMIT),
    )(activations, upstream)


def token_copies(col, own, sib, x_all, g_all, x_sem, g_sem, tokens, part):
    x_copies, g_copies = ([], []), ([], [])
    for side, group in enumerate((own, sib)):
        for k in range(8):
            rows, cols = pl.ds(side * tokens, tokens), pl.ds(column_of(col, k, part), part)
            slot = side * 8 + k
            x_copies[side].append(
                pltpu.make_async_copy(
                    group[k].at[:, pl.ds(0, part)], x_all.at[rows, cols], x_sem.at[slot]
                )
            )
            g_copies[side].append(
                pltpu.make_async_copy(
                    group[k].at[:, pl.ds(part, part)], g_all.at[rows, cols], g_sem.at[slot]
                )
            )
    return x_copies, g_copies


def w_in_copies(weights, w_in, sem, part, half):
    blocks = half // part
    return [
        pltpu.make_async_copy(
            weights.at[c, pl.ds(q * part, part)],
            w_in.at[pl.ds(c * part, part), pl.ds(q * part, part)],
            sem.at[c * blocks + q],
        )
        for c in range(8)
        for q in range(blocks)
    ]


def start(*groups):
    for group in groups:
        for copy in group:
            copy.start()


def wait(*groups):
    for group in groups:
        for copy in group:
            copy.wait()


TILES = ((0, 384), (384, 256), (640, 384), (1024, 256))


def forward_kernel(place, *refs, tokens, part, half):
    own, sib, weights = refs[:8], refs[8:16], refs[16]
    dpre_ref, terms_ref = refs[17:19]
    x_all, g_all, w_in, w_out, both, terms, x_sem, g_sem, w_sem, v_sem, out_sem = refs[19:]
    x_copies, g_copies = token_copies(
        place[1], own, sib, x_all, g_all, x_sem, g_sem, tokens, part
    )
    w_copies = w_in_copies(weights, w_in, w_sem, part, half)
    v_copies = [
        pltpu.make_async_copy(
            weights.at[c, pl.ds(half, half)], w_out.at[:, pl.ds(c * part, part)], v_sem.at[c]
        )
        for c in range(8)
    ]
    start(w_copies, x_copies[0])
    wait(w_copies)
    start(v_copies, g_copies[0])
    wait(x_copies[0])
    for side in range(2):
        rows = pl.ds(side * tokens, tokens)
        pre = jnp.dot(x_all[rows, :], w_in[...], preferred_element_type=jnp.float32)
        if side == 0:
            wait(v_copies)
            start(x_copies[1])
            wait(g_copies[0])
            start(g_copies[1])
        back = lax.dot_general(
            g_all[rows, :], w_out[...], (((1,), (1,)), ((), ())), preferred_element_type=jnp.float32
        )
        square = pre * pre
        weight = 0.5 + 0.5 * jnp.tanh(pre * (ROOT_2_PI + (ROOT_2_PI * CUBIC) * square))
        act = pre * weight
        slope = weight + act * (1.0 - weight) * (
            2.0 * ROOT_2_PI + (6.0 * ROOT_2_PI * CUBIC) * square
        )
        dpre = (back * slope).astype(jnp.bfloat16)
        dpre_ref[rows, :] = dpre
        both[pl.ds(0, half), rows] = dpre.T
        both[pl.ds(half, half), rows] = act.astype(jnp.bfloat16).T
        if side == 0:
            wait(x_copies[1], g_copies[1])

    outs = []
    for c in range(8):
        cols = pl.ds(c * part, part)
        for n, source in enumerate((x_all, g_all)):
            rows = pl.ds(n * half, half)
            terms[c, rows, :] = jnp.dot(
                both[rows, :], source[:, cols], preferred_element_type=jnp.float32
            ).astype(jnp.bfloat16)
        outs.append(pltpu.make_async_copy(terms.at[c], terms_ref.at[c], out_sem.at[c]))
        outs[-1].start()
    wait(outs)


def forward(place, own, sib, weights):
    tokens, part = own[0].shape[0], own[0].shape[1] // 2
    half = weights.shape[1] // 2
    width = 8 * part
    bf16 = jnp.bfloat16
    return pl.pallas_call(
        functools.partial(forward_kernel, tokens=tokens, part=part, half=half),
        out_shape=[
            pltpu.VMEM((2 * tokens, half), bf16),
            pltpu.HBM((8, 2 * half, part), bf16),
        ],
        in_specs=[smem()] + [hbm()] * 17,
        out_specs=[vmem(), hbm()],
        scratch_shapes=[
            pltpu.VMEM((2 * tokens, width), bf16),
            pltpu.VMEM((2 * tokens, width), bf16),
            pltpu.VMEM((width, half), bf16),
            pltpu.VMEM((half, width), bf16),
            pltpu.VMEM((2 * half, 2 * tokens), bf16),
            pltpu.VMEM((8, 2 * half, part), bf16),
            pltpu.SemaphoreType.DMA((16,)),
            pltpu.SemaphoreType.DMA((16,)),
            pltpu.SemaphoreType.DMA((8 * (half // part),)),
            pltpu.SemaphoreType.DMA((8,)),
            pltpu.SemaphoreType.DMA((8,)),
        ],
        compiler_params=pltpu.CompilerParams(vmem_limit_bytes=VMEM_LIMIT),
        cost_estimate=pl.CostEstimate(
            flops=16 * tokens * width * half,
            bytes_accessed=8 * tokens * width + 12 * half * width,
            transcendentals=2 * tokens * half,
        ),
    )(place, *own, *sib, pltpu.with_memory_space_constraint(weights, pltpu.HBM))


def input_kernel(place, dpre, weights, out_ref, w_in, sem, *, side, part, half):
    col = place[1]
    tokens = out_ref.shape[1]
    copies = w_in_copies(weights, w_in, sem, part, half)
    start(copies)
    wait(copies)
    for k in range(8):
        out_ref[k & 3, :, pl.ds((k >> 2) * part, part)] = lax.dot_general(
            dpre[pl.ds(side * tokens, tokens), :],
            w_in[pl.ds(column_of(col, k, part), part), :],
            (((1,), (1,)), ((), ())),
            preferred_element_type=jnp.float32,
        ).astype(jnp.bfloat16)


def input_terms(place, dpre, weights, side):
    tokens, half = dpre.shape[0] // 2, dpre.shape[1]
    part = weights.shape[2]
    return pl.pallas_call(
        functools.partial(input_kernel, side=side, part=part, half=half),
        out_shape=jax.ShapeDtypeStruct((4, tokens, 2 * part), jnp.bfloat16),
        in_specs=[smem(), vmem(), hbm()],
        out_specs=vmem(),
        scratch_shapes=[
            pltpu.VMEM((8 * part, half), jnp.bfloat16),
            pltpu.SemaphoreType.DMA((8 * (half // part),)),
        ],
        compiler_params=pltpu.CompilerParams(vmem_limit_bytes=24 * 1024 * 1024),
        cost_estimate=pl.CostEstimate(
            flops=16 * half * tokens * part,
            bytes_accessed=2 * tokens * half + 16 * (half + tokens) * part,
            transcendentals=0,
        ),
    )(
        place,
        pltpu.with_memory_space_constraint(dpre, pltpu.VMEM),
        pltpu.with_memory_space_constraint(weights, pltpu.HBM),
    )


def output_kernel(place, *refs):
    (share, away, other_share, other_away), (in_ref, out_ref) = refs[:4], refs[4:]
    half = share.shape[0] // 2
    core = place[2]
    for at, near, far in ((core, share, away), (1 - core, other_share, other_away)):
        at = pl.ds(pl.multiple_of(at * half, half), half)
        total = near[...].astype(jnp.float32) + far[...].astype(jnp.float32)
        in_ref[:, at] = total[:half].T
        out_ref[at, :] = total[half:]


def weight_outputs(place, *shares):
    double, part = shares[0].shape
    return pl.pallas_call(
        output_kernel,
        out_shape=(
            jax.ShapeDtypeStruct((part, double), jnp.float32),
            jax.ShapeDtypeStruct((double, part), jnp.float32),
        ),
        in_specs=[smem()] + [vmem()] * 4,
        out_specs=(vmem(), vmem()),
        compiler_params=pltpu.CompilerParams(vmem_limit_bytes=VMEM_LIMIT),
    )(place, *shares)


def add(*terms):
    total = terms[0].astype(jnp.float32)
    for term in terms[1:]:
        total = total + term.astype(jnp.float32)
    return total


def on_device(activations, weight_in, weight_out, upstream):
    tokens, part = activations.shape
    core = lax.axis_index("depth") % 2
    first = core == 0
    place = jnp.stack([lax.axis_index("row"), lax.axis_index("col"), core]).astype(jnp.int32)
    bf16 = jnp.bfloat16

    def swap(chunk):
        return lax.ppermute(chunk, "depth", CORE)

    def across(up, down):
        return lax.ppermute(
            jnp.where(first, up, down), ("depth", "col"), by_core(along_x(-1), along_x(1))
        )

    packed = pack_weights(place, weight_in, weight_out)
    weights = lax.all_gather(packed, "row", axis=0, tiled=False)
    mine = pack_tokens(activations, after(upstream, packed))

    own = {0: mine}
    own[1] = lax.ppermute(mine, "col", along_x(-1))
    own[3] = lax.ppermute(mine, "col", along_x(1))
    own[4] = lax.ppermute(mine, "col", Y_LO)
    sib = {0: swap(mine)}
    own[5] = lax.ppermute(own[4], "col", along_x(-1))
    own[7] = lax.ppermute(own[4], "col", along_x(1))
    own[2] = across(after(own[1], own[4]), own[3])
    for k in (1, 3, 4):
        sib[k] = swap(after(own[k], own[1], own[3], own[4]))
    own[6] = across(own[5], own[7])
    for k in (5, 7, 2):
        sib[k] = swap(after(own[k], own[5], own[7]))
    sib[6] = swap(own[6])
    own, sib = [[group[k] for k in range(8)] for group in (own, sib)]

    dpre, terms = forward(place, own, sib, weights)

    shares = lax.psum_scatter(terms, "row", scatter_dimension=0, tiled=False)
    theirs = swap(input_terms(place, dpre, weights, 1))
    joined = add(input_terms(place, dpre, weights, 0), theirs).astype(bf16)
    moved = [lax.ppermute(joined[k], "col", along_x(k)) for k in (2, 1, 3)]
    total = add(joined[0], *moved)
    passed = lax.ppermute(total[:, part:].astype(bf16), "col", Y_LO)
    grad_input = add(total[:, :part], passed).astype(bf16)

    shares = after(shares, grad_input)
    away = lax.ppermute(shares, "depth", Y_HI)
    grad_weight_in, grad_weight_out = weight_outputs(place, shares, away, swap(shares), swap(away))
    return (grad_input, grad_weight_in, grad_weight_out)


def solution(mesh):
    return jax.shard_map(
        on_device,
        mesh=mesh,
        in_specs=(
            P(("depth", "row"), "col"),
            P("row", "col"),
            P("col", "row"),
            P(("depth", "row"), "col"),
        ),
        out_specs=(P(("depth", "row"), "col"), P("row", "col"), P("col", "row")),
        check_vma=False,
    )
```

```python
import functools

import jax
import jax.numpy as jnp
from jax import lax
from jax.experimental import pallas as pl
from jax.experimental.pallas import tpu as pltpu
from jax.sharding import PartitionSpec as P

VMEM_LIMIT = 60 * 1024 * 1024
ROOT_2_PI = 0.7978845608028654
CUBIC = 0.044715

CORE = [(d, d ^ 1) for d in range(4)]
Y_HI = [(d, d ^ 2) for d in range(4)]
Y_LO = [(c, c ^ 4) for c in range(8)]


def along_x(step):
    return [(c, (c & 4) | ((c + step) & 3)) for c in range(8)]


def along_z(step):
    return [(z, (z + step) % 8) for z in range(8)]


def by_core(first, second):
    return [
        (d * 8 + a, d * 8 + b) for d in range(4) for a, b in (first if d % 2 == 0 else second)
    ]


def after(value, *others):
    return lax.optimization_barrier((value, *others))[0]


def hbm():
    return pl.BlockSpec(memory_space=pl.ANY)


def vmem():
    return pl.BlockSpec(memory_space=pltpu.VMEM)


def smem():
    return pl.BlockSpec(memory_space=pltpu.SMEM)


def chunk_of(z, rel, size):
    return pl.multiple_of(((z + rel) & 7) * size, size)


def column_of(col, k, size):
    return pl.multiple_of(((col & 4) ^ (4 * (k >> 2)) | ((col + k) & 3)) * size, size)


def weights_kernel(place, weight_in, weight_out, packed):
    part = weight_in.shape[0]
    half = packed.shape[0] // 2
    at = pl.multiple_of(place[2] * half, half)
    for q in range(half // part):
        packed[pl.ds(q * part, part), :] = weight_in[:, pl.ds(pl.multiple_of(at + q * part, part), part)]
    packed[pl.ds(half, half), :] = weight_out[pl.ds(at, half), :]


def pack_weights(place, weight_in, weight_out):
    part, half = weight_in.shape[0], weight_in.shape[1] // 2
    return pl.pallas_call(
        weights_kernel,
        out_shape=jax.ShapeDtypeStruct((2 * half, part), jnp.bfloat16),
        in_specs=[smem(), vmem(), vmem()],
        out_specs=vmem(),
        compiler_params=pltpu.CompilerParams(vmem_limit_bytes=VMEM_LIMIT),
    )(place, weight_in, weight_out)


def tokens_kernel(activations, upstream, mine):
    part = activations.shape[1]
    mine[:, pl.ds(0, part)] = activations[...]
    mine[:, pl.ds(part, part)] = upstream[...]


def pack_tokens(activations, upstream):
    tokens, part = activations.shape
    return pl.pallas_call(
        tokens_kernel,
        out_shape=jax.ShapeDtypeStruct((tokens, 2 * part), jnp.bfloat16),
        in_specs=[vmem(), vmem()],
        out_specs=vmem(),
        compiler_params=pltpu.CompilerParams(vmem_limit_bytes=VMEM_LIMIT),
    )(activations, upstream)


def token_copies(col, own, sib, x_all, g_all, x_sem, g_sem, tokens, part):
    x_copies, g_copies = ([], []), ([], [])
    for side, group in enumerate((own, sib)):
        for k in range(8):
            rows, cols = pl.ds(side * tokens, tokens), pl.ds(column_of(col, k, part), part)
            slot = side * 8 + k
            x_copies[side].append(
                pltpu.make_async_copy(
                    group[k].at[:, pl.ds(0, part)], x_all.at[rows, cols], x_sem.at[slot]
                )
            )
            g_copies[side].append(
                pltpu.make_async_copy(
                    group[k].at[:, pl.ds(part, part)], g_all.at[rows, cols], g_sem.at[slot]
                )
            )
    return x_copies, g_copies


def w_in_copies(weights, w_in, sem, part, half):
    blocks = half // part
    return [
        pltpu.make_async_copy(
            weights.at[c, pl.ds(q * part, part)],
            w_in.at[pl.ds(c * part, part), pl.ds(q * part, part)],
            sem.at[c * blocks + q],
        )
        for c in range(8)
        for q in range(blocks)
    ]


def start(*groups):
    for group in groups:
        for copy in group:
            copy.start()


def wait(*groups):
    for group in groups:
        for copy in group:
            copy.wait()


TILES = ((0, 384), (384, 256), (640, 384), (1024, 256))


def forward_kernel(place, *refs, tokens, part, half):
    own, sib, weights = refs[:8], refs[8:16], refs[16]
    dpre_ref, terms_ref = refs[17:19]
    x_all, g_all, w_in, w_out, both, terms, x_sem, g_sem, w_sem, v_sem, out_sem = refs[19:]
    x_copies, g_copies = token_copies(
        place[1], own, sib, x_all, g_all, x_sem, g_sem, tokens, part
    )
    w_copies = w_in_copies(weights, w_in, w_sem, part, half)
    v_copies = [
        pltpu.make_async_copy(
            weights.at[c, pl.ds(half, half)], w_out.at[:, pl.ds(c * part, part)], v_sem.at[c]
        )
        for c in range(8)
    ]
    start(w_copies, x_copies[0])
    wait(w_copies)
    start(v_copies, g_copies[0])
    wait(x_copies[0])
    for side in range(2):
        rows = pl.ds(side * tokens, tokens)
        pre = jnp.dot(x_all[rows, :], w_in[...], preferred_element_type=jnp.float32)
        if side == 0:
            wait(v_copies)
            start(x_copies[1])
            wait(g_copies[0])
            start(g_copies[1])
        back = lax.dot_general(
            g_all[rows, :], w_out[...], (((1,), (1,)), ((), ())), preferred_element_type=jnp.float32
        )
        square = pre * pre
        weight = 0.5 + 0.5 * jnp.tanh(pre * (ROOT_2_PI + (ROOT_2_PI * CUBIC) * square))
        act = pre * weight
        slope = weight + act * (1.0 - weight) * (
            2.0 * ROOT_2_PI + (6.0 * ROOT_2_PI * CUBIC) * square
        )
        dpre = (back * slope).astype(jnp.bfloat16)
        dpre_ref[rows, :] = dpre
        both[pl.ds(0, half), rows] = dpre.T
        both[pl.ds(half, half), rows] = act.astype(jnp.bfloat16).T
        if side == 0:
            wait(x_copies[1], g_copies[1])

    outs = []
    for c in range(8):
        cols = pl.ds(c * part, part)
        for n, source in enumerate((x_all, g_all)):
            rows = pl.ds(n * half, half)
            terms[c, rows, :] = jnp.dot(
                both[rows, :], source[:, cols], preferred_element_type=jnp.float32
            ).astype(jnp.bfloat16)
        outs.append(pltpu.make_async_copy(terms.at[c], terms_ref.at[c], out_sem.at[c]))
        outs[-1].start()
    wait(outs)


def forward(place, own, sib, weights):
    tokens, part = own[0].shape[0], own[0].shape[1] // 2
    half = weights.shape[1] // 2
    width = 8 * part
    bf16 = jnp.bfloat16
    return pl.pallas_call(
        functools.partial(forward_kernel, tokens=tokens, part=part, half=half),
        out_shape=[
            pltpu.VMEM((2 * tokens, half), bf16),
            pltpu.HBM((8, 2 * half, part), bf16),
        ],
        in_specs=[smem()] + [hbm()] * 17,
        out_specs=[vmem(), hbm()],
        scratch_shapes=[
            pltpu.VMEM((2 * tokens, width), bf16),
            pltpu.VMEM((2 * tokens, width), bf16),
            pltpu.VMEM((width, half), bf16),
            pltpu.VMEM((half, width), bf16),
            pltpu.VMEM((2 * half, 2 * tokens), bf16),
            pltpu.VMEM((8, 2 * half, part), bf16),
            pltpu.SemaphoreType.DMA((16,)),
            pltpu.SemaphoreType.DMA((16,)),
            pltpu.SemaphoreType.DMA((8 * (half // part),)),
            pltpu.SemaphoreType.DMA((8,)),
            pltpu.SemaphoreType.DMA((8,)),
        ],
        compiler_params=pltpu.CompilerParams(vmem_limit_bytes=VMEM_LIMIT),
        cost_estimate=pl.CostEstimate(
            flops=16 * tokens * width * half,
            bytes_accessed=8 * tokens * width + 12 * half * width,
            transcendentals=2 * tokens * half,
        ),
    )(place, *own, *sib, pltpu.with_memory_space_constraint(weights, pltpu.HBM))


def input_kernel(place, dpre, weights, out_ref, w_in, sem, *, side, part, half):
    col = place[1]
    tokens = out_ref.shape[1]
    copies = w_in_copies(weights, w_in, sem, part, half)
    start(copies)
    wait(copies)
    for k in range(8):
        out_ref[k & 3, :, pl.ds((k >> 2) * part, part)] = lax.dot_general(
            dpre[pl.ds(side * tokens, tokens), :],
            w_in[pl.ds(column_of(col, k, part), part), :],
            (((1,), (1,)), ((), ())),
            preferred_element_type=jnp.float32,
        ).astype(jnp.bfloat16)


def input_terms(place, dpre, weights, side):
    tokens, half = dpre.shape[0] // 2, dpre.shape[1]
    part = weights.shape[2]
    return pl.pallas_call(
        functools.partial(input_kernel, side=side, part=part, half=half),
        out_shape=jax.ShapeDtypeStruct((4, tokens, 2 * part), jnp.bfloat16),
        in_specs=[smem(), vmem(), hbm()],
        out_specs=vmem(),
        scratch_shapes=[
            pltpu.VMEM((8 * part, half), jnp.bfloat16),
            pltpu.SemaphoreType.DMA((8 * (half // part),)),
        ],
        compiler_params=pltpu.CompilerParams(vmem_limit_bytes=24 * 1024 * 1024),
        cost_estimate=pl.CostEstimate(
            flops=16 * half * tokens * part,
            bytes_accessed=2 * tokens * half + 16 * (half + tokens) * part,
            transcendentals=0,
        ),
    )(
        place,
        pltpu.with_memory_space_constraint(dpre, pltpu.VMEM),
        pltpu.with_memory_space_constraint(weights, pltpu.HBM),
    )


def output_kernel(place, here, other_share, other_away, in_ref, out_ref):
    half = here.shape[0] // 2
    core = place[2]
    there = other_share[...].astype(jnp.float32) + other_away[...].astype(jnp.float32)
    for at, total in ((core, here[...]), (1 - core, there)):
        at = pl.ds(pl.multiple_of(at * half, half), half)
        in_ref[:, at] = total[:half].T
        out_ref[at, :] = total[half:]


def weight_outputs(place, *shares):
    double, part = shares[0].shape
    return pl.pallas_call(
        output_kernel,
        out_shape=(
            jax.ShapeDtypeStruct((part, double), jnp.float32),
            jax.ShapeDtypeStruct((double, part), jnp.float32),
        ),
        in_specs=[smem()] + [vmem()] * 3,
        out_specs=(vmem(), vmem()),
        compiler_params=pltpu.CompilerParams(vmem_limit_bytes=32 * 1024 * 1024),
    )(place, *[pltpu.with_memory_space_constraint(share, pltpu.VMEM) for share in shares])


def add(*terms):
    total = terms[0].astype(jnp.float32)
    for term in terms[1:]:
        total = total + term.astype(jnp.float32)
    return total


def on_device(activations, weight_in, weight_out, upstream):
    tokens, part = activations.shape
    core = lax.axis_index("depth") % 2
    first = core == 0
    place = jnp.stack([lax.axis_index("row"), lax.axis_index("col"), core]).astype(jnp.int32)
    bf16 = jnp.bfloat16

    def swap(chunk):
        return lax.ppermute(chunk, "depth", CORE)

    def across(up, down):
        return lax.ppermute(
            jnp.where(first, up, down), ("depth", "col"), by_core(along_x(-1), along_x(1))
        )

    packed = pack_weights(place, weight_in, weight_out)
    weights = lax.all_gather(packed, "row", axis=0, tiled=False)
    mine = pack_tokens(activations, after(upstream, packed))

    own = {0: mine}
    own[1] = lax.ppermute(mine, "col", along_x(-1))
    own[3] = lax.ppermute(mine, "col", along_x(1))
    own[4] = lax.ppermute(mine, "col", Y_LO)
    sib = {0: swap(mine)}
    own[5] = lax.ppermute(own[4], "col", along_x(-1))
    own[7] = lax.ppermute(own[4], "col", along_x(1))
    own[2] = across(after(own[1], own[4]), own[3])
    for k in (1, 3, 4):
        sib[k] = swap(after(own[k], own[1], own[3], own[4]))
    own[6] = across(own[5], own[7])
    for k in (5, 7, 2):
        sib[k] = swap(after(own[k], own[5], own[7]))
    sib[6] = swap(own[6])
    own, sib = [[group[k] for k in range(8)] for group in (own, sib)]

    dpre, terms = forward(place, own, sib, weights)

    shares = lax.psum_scatter(terms, "row", scatter_dimension=0, tiled=False)
    theirs = swap(input_terms(place, dpre, weights, 1))
    joined = add(input_terms(place, dpre, weights, 0), theirs).astype(bf16)
    moved = [lax.ppermute(joined[k], "col", along_x(k)) for k in (2, 1, 3)]
    total = add(joined[0], *moved)
    passed = lax.ppermute(total[:, part:].astype(bf16), "col", Y_LO)
    grad_input = add(total[:, :part], passed).astype(bf16)

    shares = after(shares, grad_input)
    away = lax.ppermute(shares, "depth", Y_HI)
    grad_weight_in, grad_weight_out = weight_outputs(
        place, add(shares, away), swap(shares), swap(away)
    )
    return (grad_input, grad_weight_in, grad_weight_out)


def solution(mesh):
    return jax.shard_map(
        on_device,
        mesh=mesh,
        in_specs=(
            P(("depth", "row"), "col"),
            P("row", "col"),
            P("col", "row"),
            P(("depth", "row"), "col"),
        ),
        out_specs=(P(("depth", "row"), "col"), P("row", "col"), P("col", "row")),
        check_vma=False,
    )
```
